256 devices in a mesh: pair: 16 (over y, x_hi, core), virt: 16 (over z, x_lo).
Axes of the slice: x: 4 (x_hi: 2, x_lo: 2; x = x_hi * 2 + x_lo), y: 4, z: 8, core: 2. Of those that a mesh axis runs over, the one named last changes fastest.
Arguments:
- amplitudes: bfloat16 [256, 8, 128, 128], P('pair', None, 'virt'), may hold values from -6 to 6
- integrals: bfloat16 [96, 128, 8, 128, 128], P('pair', None, None, 'virt'), may hold values from -0.015625 to 0.015625
- pattern: int32 [8], replicated, may hold values from 0 to 7, as said below
- block_sizes: int32 [8], replicated, may hold values from 1 to 128, as said below
- pair_source: int32 [512], replicated, may hold values from 0 to 511, each once
Outputs:
- residual: float32 [512, 96, 128], P('pair', 'virt')
The draws below stay inside these ranges and needn't reach their ends.
Inputs may be any that keep to these rules, and one draw needn't show every extreme that they name: pattern[pattern[C]] = C and pattern[C] != C. `block_sizes`: the sizes sum to 700.
All inputs are finite; a program needn't handle non-finite values.
Results may differ from the reference program's by a relative error of at most 0.0003.
Values may be sent and summed in bfloat16 or wider, within the bound.
A program may use at most 128 MiB of HBM per device.

```python
import jax
import jax.numpy as jnp
from jax import lax

BW = 128
NB = 8
NVIRT = 700
PAIRS = 512
STORED = 256
ROWS = 96


def draw_pattern(key, part):
    key = jax.random.fold_in(key, 11)
    order = jax.random.permutation(key, NB).astype(jnp.int32)
    mates = order[jnp.arange(NB, dtype=jnp.int32) ^ 1]
    return jnp.zeros((NB,), jnp.int32).at[order].set(mates)


def draw_block_sizes(key, part):
    key = jax.random.fold_in(key, 23)
    small_key, moves_key, place_key = jax.random.split(key, 3)
    others = NB - 2
    small = jax.random.randint(small_key, (), 1, 4, dtype=jnp.int32)
    rest = NVIRT - BW - small
    base = rest // others
    extra = rest % others
    slots = jnp.arange(others, dtype=jnp.int32)
    sizes = base + (slots < extra).astype(jnp.int32)
    reach = jnp.minimum(base - 1, BW - base - 1)
    moves = jax.random.randint(moves_key, (others // 2,), -reach, reach + 1, dtype=jnp.int32)
    delta = jnp.stack([moves, -moves], axis=1).reshape(others)
    sizes = sizes + delta
    whole = jnp.concatenate([jnp.full((1,), BW, jnp.int32), small.reshape(1), sizes]).astype(jnp.int32)
    order = jax.random.permutation(place_key, NB).astype(jnp.int32)
    return jnp.take(whole, order).astype(jnp.int32)


def levels(own_key, dims, cuts, smallest, top_value):
    loudness, own = 1.0, jax.random.fold_in(own_key, 6)
    for dim, shards_of in cuts:
        draws = jnp.exp(jax.random.uniform(jax.random.fold_in(own, dim), (shards_of,), jnp.float32, smallest / len(cuts), top_value / len(cuts)))
        loudness = loudness * jnp.repeat(draws, dims[dim] // shards_of).reshape([-1 if axis == dim else 1 for axis in range(len(dims))])
    return loudness


def noise(own_key, dims, deviation, most, cuts=(), held_as=jnp.bfloat16):
    factor_of = levels(own_key, dims, cuts, -0.22, 0.18) if cuts else 1.0
    result = jax.random.normal(own_key, dims, jnp.float32) * deviation * factor_of
    return jnp.minimum(jnp.maximum(result, -most), most).astype(held_as)


def setup_inputs(seed: int = 0) -> dict:
    keys = jax.random.split(jax.random.key(seed), 6)
    amplitudes = noise(keys[0], (STORED, NB, BW, BW), 1.0, 6.0, ((0, 16), (2, 16)))
    integrals = noise(keys[1], (ROWS, BW, NB, BW, BW), (NB * BW * BW) ** -0.5, 0.015625, ((0, 16), (3, 16)))
    pattern = draw_pattern(jax.random.fold_in(keys[5], 71), 0)
    block_sizes = draw_block_sizes(jax.random.fold_in(keys[5], 71), 0)
    pair_source = jax.random.permutation(keys[4], PAIRS).astype(jnp.int32)
    return dict(amplitudes=amplitudes, integrals=integrals, pattern=pattern, block_sizes=block_sizes, pair_source=pair_source)


def reference(amplitudes, integrals, pattern, block_sizes, pair_source):
    flipped = jnp.swapaxes(jnp.take(amplitudes, pattern, axis=1), 2, 3)
    generated = jnp.stack([amplitudes, flipped], axis=1).reshape(PAIRS, NB, BW, BW)
    chosen = jnp.take(generated, pair_source, axis=0)
    slots = jnp.arange(BW, dtype=jnp.int32)
    row_live = slots[None, :] < block_sizes[:, None]
    col_live = slots[None, :] < jnp.take(block_sizes, pattern)[:, None]
    live_mask = (row_live[:, :, None] & col_live[:, None, :]).astype(jnp.bfloat16)
    chosen = chosen * live_mask[None]
    flat = chosen.reshape(PAIRS, NB * BW * BW)

    def one_row(slab_row):
        return jnp.dot(flat, slab_row.reshape(BW, NB * BW * BW).T, preferred_element_type=jnp.float32)

    partial_rows = lax.map(one_row, integrals)
    total = jnp.transpose(partial_rows, (1, 0, 2))
    rows = jnp.arange(ROWS, dtype=jnp.int32)
    blocks = rows % NB
    offsets = rows // NB
    a_live = offsets < jnp.take(block_sizes, blocks)
    b_live = slots[None, :] < jnp.take(block_sizes, jnp.take(pattern, blocks))[:, None]
    out_mask = (a_live[:, None] & b_live).astype(jnp.float32)
    return total * out_mask[None]
```

```python
import jax
import jax.numpy as jnp
from jax import lax
from jax.sharding import PartitionSpec as P


def on_device(amplitudes, integrals, pattern, block_sizes, pair_source):
    stored, blocks, slice_rows, width = amplitudes.shape
    row_dev = integrals.shape[0]
    virt_count = lax.axis_size("virt")
    flat_len = blocks * slice_rows * width
    columns = lax.all_to_all(amplitudes, "virt", split_axis=3, concat_axis=2, tiled=True)
    flipped = jnp.swapaxes(jnp.take(columns, pattern, axis=1), 2, 3)
    slice_start = lax.axis_index("virt") * slice_rows
    own_slots = slice_start + jnp.arange(slice_rows, dtype=jnp.int32)
    row_live = own_slots[None, :] < block_sizes[:, None]
    all_slots = jnp.arange(width, dtype=jnp.int32)
    col_live = all_slots[None, :] < jnp.take(block_sizes, pattern)[:, None]
    live_mask = (row_live[:, :, None] & col_live[:, None, :]).astype(jnp.bfloat16)
    generated = jnp.stack([amplitudes, flipped], axis=1) * live_mask[None, None]
    generated = generated.reshape(2 * stored, flat_len)
    everything = lax.all_gather(generated, "pair", axis=0, tiled=True)
    slab = integrals.reshape(row_dev * width, flat_len)
    partial_value = lax.dot_general(
        everything, slab, (((1,), (1,)), ((), ())), preferred_element_type=jnp.float32
    )
    partial_value = jnp.take(partial_value, pair_source, axis=0)
    mine = lax.psum_scatter(partial_value, "virt", scatter_dimension=0, tiled=True)
    count = virt_count
    perm = [(p * count + v, v * count + p) for p in range(count) for v in range(count)]
    mine = lax.ppermute(mine, ("pair", "virt"), perm)
    mine = mine.reshape(mine.shape[0], row_dev, width)
    rows = lax.axis_index("virt") * row_dev + jnp.arange(row_dev, dtype=jnp.int32)
    row_blocks = rows % blocks
    offsets = rows // blocks
    a_live = offsets < jnp.take(block_sizes, row_blocks)
    b_live = all_slots[None, :] < jnp.take(block_sizes, jnp.take(pattern, row_blocks))[:, None]
    out_mask = a_live[:, None] & b_live
    return jnp.where(out_mask[None], mine, 0.0)


def solution(mesh):
    return jax.shard_map(
        on_device,
        mesh=mesh,
        in_specs=(
            P("pair", None, "virt", None),
            P("pair", None, None, "virt", None),
            P(),
            P(),
            P(),
        ),
        out_specs=P("pair", "virt", None),
        check_vma=False,
    )
```

```python
import functools

import jax
import jax.numpy as jnp
from jax import lax
from jax.experimental import pallas as pl
from jax.experimental.pallas import tpu as pltpu
from jax.sharding import PartitionSpec as P

MESH = pl.DeviceIdType.MESH
BF, F32 = jnp.bfloat16, jnp.float32
NB, SL, BW = 8, 8, 128
QS, PD, RD = 16, 32, 6
RB = RD * BW
CHUNK = 64
KP = 2 * NB * BW
FAR = (4, 3, 5, 2, 6, 1, 7)


def ladder_kernel(amp, integrals, pattern, sizes, source, out, slab, wide, basis, gathered, total, ordered, from_x, from_z, pieces,
                  staged, mixed, sent, landed, turned, summed, final,
                  slab_sem, a2a_send, a2a_recv, gat_send, gat_recv, x_send, x_recv, z_send, z_recv, fin_send, fin_recv):
    p, v = lax.axis_index("pair"), lax.axis_index("virt")
    y, h, core = p // 4, (p // 2) % 2, p % 2
    z, xl = v // 2, v % 2

    def pair_of(dy, dh, dc):
        return (((y + dy) % 4) * 2 + (h + dh) % 2) * 2 + (core + dc) % 2

    up, down, across, sibling = pair_of(1, 0, 0), pair_of(3, 0, 0), pair_of(0, 1, 0), pair_of(0, 0, 1)

    loads = []
    for k in range(RB // CHUNK):
        rows = pl.ds(k * CHUNK * NB * SL, CHUNK * NB * SL)
        load = pltpu.make_async_copy(integrals.at[rows], slab.at[rows], slab_sem.at[k])
        load.start()
        loads.append(load)

    barrier = pltpu.get_barrier_semaphore()
    for q in (up, down, across, sibling):
        pl.semaphore_signal(barrier, inc=1, device_id=(q, v), device_id_type=MESH)
    for j in range(1, 16):
        pl.semaphore_signal(barrier, inc=1, device_id=(p, (v + j) % 16), device_id_type=MESH)

    @pl.when(p != v)
    def _():
        pl.semaphore_signal(barrier, inc=1, device_id=(v, p), device_id_type=MESH)
        pl.semaphore_wait(barrier, 20)

    @pl.when(p == v)
    def _():
        pl.semaphore_wait(barrier, 19)

    lane = lax.broadcasted_iota(jnp.int32, (1, BW), 1)

    def mate_size(block):
        mate, partner = pattern[block], 0
        for other in range(NB):
            partner = jnp.where(mate == other, sizes[other], partner)
        return partner

    mate_sizes = [mate_size(block) for block in range(NB)]

    def live(block, offset):
        return lane < jnp.where(v * SL + offset < sizes[block], mate_sizes[block], 0)

    gat_sends = []

    def send(f, half, owner, q, index):
        part = pl.ds(half * 2, 2)
        copy = pltpu.make_async_remote_copy(
            src_ref=gathered.at[f, owner, part], dst_ref=gathered.at[f, owner, part],
            send_sem=gat_send.at[f, half, index], recv_sem=gat_recv.at[f, half, owner],
            device_id=(q, v), device_id_type=MESH)
        copy.start()
        gat_sends.append(copy)

    def arrived(f, half, owner):
        part = pl.ds(half * 2, 2)
        pltpu.make_async_remote_copy(
            src_ref=gathered.at[f, owner, part], dst_ref=gathered.at[f, owner, part],
            send_sem=gat_send.at[f, half, 0], recv_sem=gat_recv.at[f, half, owner],
            device_id=(p, v), device_id_type=MESH).wait_recv()

    def send_own(f):
        for half in range(2):
            for index, q in enumerate((up, down, across, sibling)):
                send(f, half, p, q, index)

    staged[...] = amp[...].astype(F32)
    for c in range(SL):
        for block in range(NB):
            piece = staged[pl.ds(block * SL + c, QS, stride=NB * SL), :]
            piece = jnp.where(live(block, c), piece, 0.0).astype(BF)
            lanes = pl.ds((c % 2) * NB * BW + block * BW, BW)
            gathered[0, p, c // 2, :, lanes] = piece
    send_own(0)

    group = lax.broadcasted_iota(jnp.int32, (SL, BW), 1) // SL

    def mix(block, carry):
        tiles = [staged[pl.ds(pl.multiple_of(q * NB * SL + block * SL, SL), SL), :] for q in range(QS)]
        for k in range(4):
            bit = 1 << k
            high = (group // bit) % 2 == 1
            new = list(tiles)
            for q in range(QS):
                if q & bit == 0:
                    new[q] = jnp.where(high, pltpu.roll(tiles[q | bit], SL * bit, 1), tiles[q])
                    new[q | bit] = jnp.where(high, tiles[q | bit], pltpu.roll(tiles[q], BW - SL * bit, 1))
            tiles = new
        for u in range(16):
            mixed[u, pl.ds(pl.multiple_of(block * SL, SL), SL), :] = tiles[u]
        return carry

    lax.fori_loop(0, NB, mix, 0)
    sent[...] = mixed[...].astype(BF)
    a2a = []
    for j in range(1, 16):
        u = (v + j) % 16
        copy = pltpu.make_async_remote_copy(
            src_ref=sent.at[u], dst_ref=landed.at[v], send_sem=a2a_send.at[j], recv_sem=a2a_recv.at[j],
            device_id=(p, u), device_id_type=MESH)
        copy.start()
        a2a.append(copy)
    landed[v] = sent[v]

    def relayout(k):
        rows = CHUNK * NB * SL
        wide[...] = slab[pl.ds(k * rows, rows), :].astype(F32)
        for c in range(SL):
            for block in range(NB):
                piece = wide[pl.ds(block * SL + c, CHUNK, stride=NB * SL), :].astype(BF)
                lanes = pl.ds((c % 2) * NB * BW + block * BW, BW)
                basis[c // 2, pl.ds(pl.multiple_of(k * CHUNK, CHUNK), CHUNK), lanes] = piece

    def relayouts(first, count):
        for k in range(first, first + count):
            loads[k].wait()

        def step(k, carry):
            relayout(k)
            return carry

        lax.fori_loop(first, first + count, step, 0)

    def event(f, half, kind):
        if kind == 0:
            owner, onward = pair_of(3, 0, 0), [(up, 4)] if half == 0 else []
        elif kind == 1:
            owner, onward = pair_of(1, 0, 0), [(down, 4)] if half == 1 else []
        elif kind == 2:
            owner, onward = across, [(up, 5), (down, 6)]
        elif kind == 3:
            owner, onward = pair_of(2, 0, 0), [(across, 7)]
        else:
            owner, onward = pair_of((3, 1, 2)[kind - 4], 1, 0), []
        arrived(f, half, owner)
        for q, index in onward:
            send(f, half, owner, q, index)
        send(f, half, owner, sibling, 8 + kind)

    def events(f, half, kinds):
        for kind in kinds:
            event(f, half, kind)

    def siblings(f, half):
        for dy in range(4):
            for dh in range(2):
                arrived(f, half, pair_of(dy, dh, 1))

    def multiply(f, half):
        rows = pl.ds(f * 256, 256)

        def step(c, carry):
            left = gathered[f, :, c].reshape(256, KP)
            part = lax.dot_general(left, basis[c], (((1,), (1,)), ((), ())), preferred_element_type=F32)
            total[rows, :] = total[rows, :] + part
            return carry

        lax.fori_loop(half * 2, half * 2 + 2, step, 0)

    relayouts(0, 2)
    events(0, 0, (0, 1, 2))
    relayouts(2, 2)
    events(0, 1, (0, 1, 2))

    for copy in a2a:
        copy.wait()
    mixed[...] = landed[...].astype(F32)
    for block in range(NB):
        mate = pattern[block]
        tile = mixed[:, pl.ds(0, SL), :]
        for other in range(1, NB):
            tile = jnp.where(mate == other, mixed[:, pl.ds(other * SL, SL), :], tile)
        turned[...] = tile.reshape(BW, BW).T
        for c in range(SL):
            piece = turned[pl.ds(c, QS, stride=SL), :]
            piece = jnp.where(live(block, c), piece, 0.0).astype(BF)
            lanes = pl.ds((c % 2) * NB * BW + block * BW, BW)
            gathered[1, p, c // 2, :, lanes] = piece
    send_own(1)

    total[...] = jnp.zeros_like(total)
    relayouts(4, 2)
    events(0, 0, (3, 4, 5, 6))
    relayouts(6, 2)
    events(0, 1, (3, 4, 5, 6))
    relayouts(8, 2)
    events(1, 0, (0, 1, 2))
    relayouts(10, 2)
    siblings(0, 0)
    events(1, 1, (0, 1, 2))
    multiply(0, 0)
    events(1, 0, (3, 4, 5, 6))
    siblings(0, 1)
    multiply(0, 1)
    events(1, 1, (3, 4, 5, 6))
    siblings(1, 0)
    multiply(1, 0)
    siblings(1, 1)
    multiply(1, 1)

    for part in range(4):
        rows = pl.ds(part * 128, 128)
        whole = total[rows, :]
        high = whole.astype(BF)
        rest = whole - high.astype(F32)
        middle = rest.astype(BF)
        pieces[0, rows, :] = high
        pieces[1, rows, :] = middle
        pieces[2, rows, :] = (rest - middle.astype(F32)).astype(BF)
    generated = lax.broadcasted_iota(jnp.int32, (PD, 512), 1)

    def reorder(owners):
        takes = []
        for owner in owners:
            g = source[pl.ds(pl.multiple_of(owner * PD, PD), PD), :]
            takes.append(jnp.where(generated == (g & 1) * 256 + (g >> 1), 1.0, 0.0))
        take = jnp.concatenate(takes, axis=0).astype(BF)
        rows = lax.dot_general(take, pieces[0], (((1,), (0,)), ((), ())), preferred_element_type=F32)
        for k in (1, 2):
            rows += lax.dot_general(take, pieces[k], (((1,), (0,)), ((), ())), preferred_element_type=F32)
        for j, owner in enumerate(owners):
            ordered[owner] = rows[j * PD:(j + 1) * PD]

    order = [(z + dz) % 8 for dz in FAR + (0,)]
    x_copies = []
    for part in (0, 4):
        reorder([u * 2 + 1 - xl for u in order[part:part + 4]])
        for j in range(part, part + 4):
            copy = pltpu.make_async_remote_copy(
                src_ref=ordered.at[order[j] * 2 + 1 - xl], dst_ref=from_x.at[j], send_sem=x_send.at[j],
                recv_sem=x_recv.at[j], device_id=(p, z * 2 + 1 - xl), device_id_type=MESH)
            copy.start()
            x_copies.append(copy)
    for part in (0, 4):
        reorder([u * 2 + xl for u in order[part:part + 4]])
    z_copies = []
    for j, dz in enumerate(FAR + (0,)):
        owner = ((z + dz) % 8) * 2 + xl
        x_copies[j].wait_recv()
        ordered[owner] = ordered[owner] + from_x[j]
        if dz:
            copy = pltpu.make_async_remote_copy(
                src_ref=ordered.at[owner], dst_ref=from_z.at[j], send_sem=z_send.at[j], recv_sem=z_recv.at[j],
                device_id=(p, owner), device_id_type=MESH)
            copy.start()
            z_copies.append(copy)
    acc = ordered[v]
    for j, copy in enumerate(z_copies):
        copy.wait_recv()
        acc = acc + from_z[j]
    summed[...] = acc

    @pl.when(p == v)
    def _():
        final[...] = summed[...]

    @pl.when(p != v)
    def _():
        copy = pltpu.make_async_remote_copy(
            src_ref=summed, dst_ref=final, send_sem=fin_send, recv_sem=fin_recv, device_id=(v, p), device_id_type=MESH)
        copy.start()
        copy.wait()

    for i in range(RD):
        row = v * RD + i
        width = 0
        for block in range(NB):
            here = jnp.where(row // NB < sizes[block], mate_sizes[block], 0)
            width = jnp.where(row % NB == block, here, width)
        lanes = pl.ds(i * BW, BW)
        out[:, lanes] = jnp.where(lane < width, final[:, lanes], 0.0)
    for copy in gat_sends + x_copies + z_copies:
        copy.wait_send()


def on_device(amplitudes, integrals, pattern, block_sizes, pair_source):
    vmem, smem = pl.BlockSpec(memory_space=pltpu.VMEM), pl.BlockSpec(memory_space=pltpu.SMEM)
    dma = pltpu.SemaphoreType.DMA
    result = pl.pallas_call(
        ladder_kernel,
        out_shape=jax.ShapeDtypeStruct((PD, RB), F32),
        in_specs=[vmem, pl.BlockSpec(memory_space=pl.ANY), smem, smem, vmem],
        out_specs=vmem,
        scratch_shapes=[
            pltpu.VMEM((RB * NB * SL, BW), BF),
            pltpu.VMEM((CHUNK * NB * SL, BW), F32),
            pltpu.VMEM((4, RB, KP), BF),
            pltpu.VMEM((2, 16, 4, QS, KP), BF),
            pltpu.VMEM((512, RB), F32),
            pltpu.VMEM((16, PD, RB), F32),
            pltpu.VMEM((8, PD, RB), F32),
            pltpu.VMEM((7, PD, RB), F32),
            pltpu.VMEM((3, 512, RB), BF),
            pltpu.VMEM((QS * NB * SL, BW), F32),
            pltpu.VMEM((16, NB * SL, BW), F32),
            pltpu.VMEM((16, NB * SL, BW), BF),
            pltpu.VMEM((16, NB * SL, BW), BF),
            pltpu.VMEM((BW, BW), F32),
            pltpu.VMEM((PD, RB), F32),
            pltpu.VMEM((PD, RB), F32),
            dma((RB // CHUNK,)),
            dma((16,)), dma((16,)),
            dma((2, 2, 16)), dma((2, 2, 16)),
            dma((8,)), dma((8,)), dma((7,)), dma((7,)),
            dma, dma,
        ],
        compiler_params=pltpu.CompilerParams(collective_id=0, has_side_effects=True, vmem_limit_bytes=60 * 2**20),
        cost_estimate=pl.CostEstimate(flops=2 * 512 * RB * 8192, bytes_accessed=14 * 2**20, transcendentals=0),
    )(amplitudes.reshape(QS * NB * SL, BW), integrals.reshape(RB * NB * SL, BW), pattern, block_sizes, pair_source.reshape(512, 1))
    return result.reshape(PD, RD, BW)


def solution(mesh):
    return jax.shard_map(
        on_device,
        mesh=mesh,
        in_specs=(P("pair", None, "virt", None), P("pair", None, None, "virt", None), P(), P(), P()),
        out_specs=P("pair", "virt", None),
        check_vma=False,
    )
```

```python
import functools

import jax
import jax.numpy as jnp
from jax import lax
from jax.experimental import pallas as pl
from jax.experimental.pallas import tpu as pltpu
from jax.sharding import PartitionSpec as P

MESH = pl.DeviceIdType.MESH
BF, F32 = jnp.bfloat16, jnp.float32
NB, SL, BW = 8, 8, 128
QS, PD, RD = 16, 32, 6
RB = RD * BW
CHUNK = 128
LANES = NB * BW
KP = 1408
WIN = 768
REACH = (((0, 6), (2, 8), (4, 8)), ((0, 6), (0, 8), (2, 8)))
FAR = (4, 3, 5, 2, 6, 1, 7)


def ladder_kernel(amp, integrals, pattern, sizes, source, out, slab, narrow, select, few, basis, gathered, total, ordered, from_x, from_z, pieces,
                  staged, mixed, sent, landed, turned, column, summed, final,
                  slab_sem, a2a_send, a2a_recv, gat_send, gat_recv, x_send, x_recv, z_send, z_recv, fin_send, fin_recv):
    p, v = lax.axis_index("pair"), lax.axis_index("virt")
    y, h, core = p // 4, (p // 2) % 2, p % 2
    z, xl = v // 2, v % 2

    def pair_of(dy, dh, dc):
        return (((y + dy) % 4) * 2 + (h + dh) % 2) * 2 + (core + dc) % 2

    up, down, across, sibling = pair_of(1, 0, 0), pair_of(3, 0, 0), pair_of(0, 1, 0), pair_of(0, 0, 1)

    def load(k):
        rows = pl.ds(pl.multiple_of(k * CHUNK * NB * SL, CHUNK * NB * SL), CHUNK * NB * SL)
        return pltpu.make_async_copy(integrals.at[rows], slab.at[rows], slab_sem.at[k])

    for k in range(RB // CHUNK):
        load(k).start()

    barrier = pltpu.get_barrier_semaphore()
    for q in (up, down, across, sibling):
        pl.semaphore_signal(barrier, inc=1, device_id=(q, v), device_id_type=MESH)
    for j in range(1, 16):
        pl.semaphore_signal(barrier, inc=1, device_id=(p, (v + j) % 16), device_id_type=MESH)

    @pl.when(p + v != 0)
    def _():
        pl.semaphore_signal(barrier, inc=1, device_id=(v, (p - v + 16) % 16), device_id_type=MESH)

    lane = lax.broadcasted_iota(jnp.int32, (1, BW), 1)

    def mate_size(block):
        mate, partner = pattern[block], 0
        for other in range(NB):
            partner = jnp.where(mate == other, sizes[other], partner)
        return partner

    mate_sizes = [mate_size(block) for block in range(NB)]

    def live(block, offset):
        return lane < jnp.where(v * SL + offset < sizes[block], mate_sizes[block], 0)

    def hop(f, slot, q, there, index):
        return pltpu.make_async_remote_copy(
            src_ref=gathered.at[f, core, slot], dst_ref=gathered.at[f, core, there],
            send_sem=gat_send.at[f, index], recv_sem=gat_recv.at[f, there], device_id=(q, v), device_id_type=MESH)

    def send_own(f):
        hop(f, 0, up, 1, 0).start()
        hop(f, 0, down, 2, 1).start()
        hop(f, 0, across, 3, 2).start()

    def arrived(f, slot):
        hop(f, slot, sibling, slot, 0).wait_recv()

    def share(f, far, from_core):
        slots = pl.ds(far * 4, 4)
        return pltpu.make_async_remote_copy(
            src_ref=gathered.at[f, from_core, slots], dst_ref=gathered.at[f, from_core, slots],
            send_sem=gat_send.at[f, 7 + far], recv_sem=gat_recv.at[f, 8 + far], device_id=(sibling, v),
            device_id_type=MESH)

    def near(f):
        arrived(f, 1)
        if f == 0:
            hop(f, 1, up, 6, 3).start()
        arrived(f, 2)
        if f == 1:
            hop(f, 2, down, 6, 3).start()
        arrived(f, 3)
        hop(f, 3, up, 4, 4).start()
        hop(f, 3, down, 5, 5).start()
        share(f, 0, core).start()

    def far(f):
        arrived(f, 6)
        hop(f, 6, across, 7, 6).start()
        arrived(f, 4)
        arrived(f, 5)
        arrived(f, 7)
        share(f, 1, core).start()

    def shared(f):
        for k in range(2):
            share(f, k, 1 - core).wait_recv()

    staged[...] = amp[...].astype(F32)

    shift = lax.broadcasted_iota(jnp.int32, (BW, WIN), 1) - lax.broadcasted_iota(jnp.int32, (BW, WIN), 0)
    depth = lax.broadcasted_iota(jnp.int32, (BW, WIN), 0)
    offset = 0
    for block in range(NB):
        inside = depth < mate_sizes[block]
        for odd in range(2):
            chosen = jnp.logical_and(inside, shift == offset + odd * (KP // 2 - (KP - WIN)))
            select[odd, pl.ds(block * BW, BW), :] = jnp.where(chosen, 1.0, 0.0).astype(BF)
        offset = offset + mate_sizes[block]

    def pack(source_ref, rows, put):
        def window(odd, part):
            first, last = REACH[odd][part]
            lanes = pl.ds(first * BW, (last - first) * BW)
            left = source_ref[odd, :, :, lanes].reshape(4 * rows, (last - first) * BW)
            right = select[odd, lanes, pl.ds(part * 256, 256)]
            return lax.dot_general(left, right, (((1,), (0,)), ((), ())), preferred_element_type=F32)

        def save(lane, value):
            value = value.astype(BF)
            for k in range(4):
                put(k, pl.ds(lane, value.shape[1]), value[k * rows:(k + 1) * rows])

        save(0, window(0, 0))
        save(256, window(0, 1))
        low = window(0, 2)
        save(512, low[:, :BW])
        high = window(1, 0)
        save(640, low[:, BW:] + high[:, :BW])
        save(768, high[:, BW:])
        save(896, window(1, 1))
        save(1152, window(1, 2))

    def pack_amplitudes(f):
        def put(k, lanes, value):
            gathered[f, core, 0, k, :, lanes] = value

        pack(few, QS, put)

    for c in range(SL):
        for block in range(NB):
            piece = staged[pl.ds(block * SL + c, QS, stride=NB * SL), :]
            piece = jnp.where(live(block, c), piece, 0.0).astype(BF)
            few[c % 2, c // 2, :, pl.ds(block * BW, BW)] = piece
    pack_amplitudes(0)

    group = lax.broadcasted_iota(jnp.int32, (SL, BW), 1) // SL

    def mix(block, carry):
        tiles = [staged[pl.ds(pl.multiple_of(q * NB * SL + block * SL, SL), SL), :] for q in range(QS)]
        for k in range(4):
            bit = 1 << k
            high = (group // bit) % 2 == 1
            new = list(tiles)
            for q in range(QS):
                if q & bit == 0:
                    new[q] = jnp.where(high, pltpu.roll(tiles[q | bit], SL * bit, 1), tiles[q])
                    new[q | bit] = jnp.where(high, tiles[q | bit], pltpu.roll(tiles[q], BW - SL * bit, 1))
            tiles = new
        for u in range(16):
            mixed[u, pl.ds(pl.multiple_of(block * SL, SL), SL), :] = tiles[u]
        return carry

    lax.fori_loop(0, NB, mix, 0)
    sent[...] = mixed[...].astype(BF)

    g = source[...]
    dy, dh = ((g >> 7) - y) & 3, ((g >> 6) - h) & 1
    slot = jnp.where(dy == 0, dh * 3, jnp.where(dy == 3, 1 + dh * 3, jnp.where(dy == 1, 2 + dh * 3, 6 + dh)))
    place = ((g & 1) * 256 + ((g >> 5) & 1) * 128 + slot * QS + ((g >> 1) & 15)).astype(F32)
    for k in range(4):
        column[pl.ds(k * BW, BW), :] = jnp.broadcast_to(place[k:k + 1, :], (BW, BW)).T.astype(jnp.int32)

    @pl.when(p + v != 0)
    def _():
        pl.semaphore_wait(barrier, 20)

    @pl.when(p + v == 0)
    def _():
        pl.semaphore_wait(barrier, 19)

    send_own(0)
    a2a = []
    for j in range(1, 16):
        u = (v + j) % 16
        copy = pltpu.make_async_remote_copy(
            src_ref=sent.at[u], dst_ref=landed.at[v], send_sem=a2a_send.at[j], recv_sem=a2a_recv.at[j],
            device_id=(p, u), device_id_type=MESH)
        copy.start()
        a2a.append(copy)
    landed[v] = sent[v]

    def relayout(k):
        rows = CHUNK * NB * SL
        w = slab[pl.ds(pl.multiple_of(k * rows, rows), rows), :].reshape(CHUNK, NB, SL, BW)
        for block in range(NB):
            t = jnp.swapaxes(w[:, block], 0, 1)
            for c in range(SL):
                narrow[c % 2, c // 2, :, pl.ds(block * BW, BW)] = t[c]

        def put(j, lanes, value):
            basis[j, pl.ds(pl.multiple_of(k * CHUNK, CHUNK), CHUNK), lanes] = value

        pack(narrow, CHUNK, put)

    def multiply(f):
        rows = pl.ds(f * 256, 256)

        def step(c, carry):
            left = gathered[f, :, :, c].reshape(256, KP)
            part = lax.dot_general(left, basis[c], (((1,), (1,)), ((), ())), preferred_element_type=F32)
            total[rows, :] = total[rows, :] + part
            return carry

        lax.fori_loop(0, 4, step, 0)

    def transposed():
        for copy in a2a:
            copy.wait()
        mixed[...] = landed[...].astype(F32)
        for block in range(NB):
            mate = pattern[block]
            tile = mixed[:, pl.ds(0, SL), :]
            for other in range(1, NB):
                tile = jnp.where(mate == other, mixed[:, pl.ds(other * SL, SL), :], tile)
            turned[...] = tile.reshape(BW, BW).T
            for c in range(SL):
                piece = turned[pl.ds(c, QS, stride=SL), :]
                piece = jnp.where(live(block, c), piece, 0.0).astype(BF)
                few[c % 2, c // 2, :, pl.ds(block * BW, BW)] = piece
        pack_amplitudes(1)
        send_own(1)

    def stage(k, carry):
        load(k).wait()
        relayout(k)

        @pl.when(k == 1)
        def _():
            near(0)

        @pl.when(k == 2)
        def _():
            transposed()

        @pl.when(k == 4)
        def _():
            far(0)

        return carry

    total[...] = jnp.zeros_like(total)
    lax.fori_loop(0, RB // CHUNK, stage, 0)
    shared(0)
    near(1)
    multiply(0)
    far(1)
    shared(1)
    multiply(1)

    for part in range(4):
        rows = pl.ds(part * 128, 128)
        whole = total[rows, :]
        high = whole.astype(BF)
        rest = whole - high.astype(F32)
        middle = rest.astype(BF)
        pieces[0, rows, :] = high
        pieces[1, rows, :] = middle
        pieces[2, rows, :] = (rest - middle.astype(F32)).astype(BF)

    def reorder(which, first, owners):
        takes = []
        for owner in owners:
            rows = pl.ds(pl.multiple_of((owner + p) % 16 * PD, PD), PD)
            takes.append(jnp.concatenate([jnp.where(column[rows, :] == lane + k * BW, 1.0, 0.0) for k in range(4)], axis=1))
        take = jnp.concatenate(takes, axis=0).astype(BF)
        rows = lax.dot_general(take, pieces[0], (((1,), (0,)), ((), ())), preferred_element_type=F32)
        for k in (1, 2):
            rows += lax.dot_general(take, pieces[k], (((1,), (0,)), ((), ())), preferred_element_type=F32)
        for j in range(4):
            ordered[which, first + j] = rows[j * PD:(j + 1) * PD]

    order = [(z + dz) % 8 for dz in FAR + (0,)]
    x_copies = []
    for part in (0, 4):
        reorder(0, part, [u * 2 + 1 - xl for u in order[part:part + 4]])
        for j in (part, part + 2):
            pieces_two = pl.ds(j, 2)
            copy = pltpu.make_async_remote_copy(
                src_ref=ordered.at[0, pieces_two], dst_ref=from_x.at[pieces_two], send_sem=x_send.at[j],
                recv_sem=x_recv.at[j], device_id=(p, z * 2 + 1 - xl), device_id_type=MESH)
            copy.start()
            x_copies.append(copy)
    for part in (0, 4):
        reorder(1, part, [u * 2 + xl for u in order[part:part + 4]])
    z_copies = []
    for j, dz in enumerate(FAR + (0,)):
        owner = ((z + dz) % 8) * 2 + xl
        if j % 2 == 0:
            x_copies[j // 2].wait_recv()
        ordered[1, j] = ordered[1, j] + from_x[j]
        if dz:
            copy = pltpu.make_async_remote_copy(
                src_ref=ordered.at[1, j], dst_ref=from_z.at[j], send_sem=z_send.at[j], recv_sem=z_recv.at[j],
                device_id=(p, owner), device_id_type=MESH)
            copy.start()
            z_copies.append(copy)
    acc = ordered[1, 7]
    for j, copy in enumerate(z_copies):
        copy.wait_recv()
        acc = acc + from_z[j]
    summed[...] = acc

    @pl.when(p + v == 0)
    def _():
        final[...] = summed[...]

    @pl.when(p + v != 0)
    def _():
        copy = pltpu.make_async_remote_copy(
            src_ref=summed, dst_ref=final, send_sem=fin_send, recv_sem=fin_recv, device_id=((p + v) % 16, p),
            device_id_type=MESH)
        copy.start()
        copy.wait()

    for i in range(RD):
        row = v * RD + i
        width = 0
        for block in range(NB):
            here = jnp.where(row // NB < sizes[block], mate_sizes[block], 0)
            width = jnp.where(row % NB == block, here, width)
        lanes = pl.ds(i * BW, BW)
        out[:, lanes] = jnp.where(lane < width, final[:, lanes], 0.0)
    for copy in x_copies + z_copies:
        copy.wait_send()

    for f in range(2):
        for index in range(7):
            hop(f, 0, sibling, 0, index).wait_send()
        for k in range(2):
            share(f, k, core).wait_send()


def on_device(amplitudes, integrals, pattern, block_sizes, pair_source):
    vmem, smem = pl.BlockSpec(memory_space=pltpu.VMEM), pl.BlockSpec(memory_space=pltpu.SMEM)
    dma = pltpu.SemaphoreType.DMA
    result = pl.pallas_call(
        ladder_kernel,
        out_shape=jax.ShapeDtypeStruct((PD, RB), F32),
        in_specs=[vmem, pl.BlockSpec(memory_space=pl.ANY), smem, smem, vmem],
        out_specs=vmem,
        scratch_shapes=[
            pltpu.VMEM((RB * NB * SL, BW), BF),
            pltpu.VMEM((2, 4, CHUNK, LANES), BF),
            pltpu.VMEM((2, LANES, WIN), BF),
            pltpu.VMEM((2, 4, QS, LANES), BF),
            pltpu.VMEM((4, RB, KP), BF),
            pltpu.VMEM((2, 2, 8, 4, QS, KP), BF),
            pltpu.VMEM((512, RB), F32),
            pltpu.VMEM((2, 8, PD, RB), F32),
            pltpu.VMEM((8, PD, RB), F32),
            pltpu.VMEM((7, PD, RB), F32),
            pltpu.VMEM((3, 512, RB), BF),
            pltpu.VMEM((QS * NB * SL, BW), F32),
            pltpu.VMEM((16, NB * SL, BW), F32),
            pltpu.VMEM((16, NB * SL, BW), BF),
            pltpu.VMEM((16, NB * SL, BW), BF),
            pltpu.VMEM((BW, BW), F32),
            pltpu.VMEM((512, BW), jnp.int32),
            pltpu.VMEM((PD, RB), F32),
            pltpu.VMEM((PD, RB), F32),
            dma((RB // CHUNK,)),
            dma((16,)), dma((16,)),
            dma((2, 9)), dma((2, 10)),
            dma((8,)), dma((8,)), dma((7,)), dma((7,)),
            dma, dma,
        ],
        compiler_params=pltpu.CompilerParams(collective_id=0, has_side_effects=True, vmem_limit_bytes=60 * 2**20),
        cost_estimate=pl.CostEstimate(flops=2 * 512 * RB * 8192, bytes_accessed=14 * 2**20, transcendentals=0),
    )(amplitudes.reshape(QS * NB * SL, BW), integrals.reshape(RB * NB * SL, BW), pattern, block_sizes, pair_source.reshape(4, BW))
    return result.reshape(PD, RD, BW)


def solution(mesh):
    return jax.shard_map(
        on_device,
        mesh=mesh,
        in_specs=(P("pair", None, "virt", None), P("pair", None, None, "virt", None), P(), P(), P()),
        out_specs=P("pair", "virt", None),
        check_vma=False,
    )
```

```python
import functools

import jax
import jax.numpy as jnp
from jax import lax
from jax.experimental import pallas as pl
from jax.experimental.pallas import tpu as pltpu
from jax.sharding import PartitionSpec as P

MESH = pl.DeviceIdType.MESH
BF, F32 = jnp.bfloat16, jnp.float32
NB, SL, BW = 8, 8, 128
QS, PD, RD = 16, 32, 6
RB = RD * BW
CHUNK = 128
LANES = NB * BW
KP = 1408
WIN = 768
REACH = (((0, 6), (2, 8), (4, 8)), ((0, 6), (0, 8), (2, 8)))
FAR = (4, 3, 5, 2, 6, 1, 7)
COLS = ((0, 512), (512, 256))


def ladder_kernel(amp, integrals, pattern, sizes, source, out, slab, narrow, select, few, basis, gathered, total, ordered_a, ordered_b, from_x_a, from_x_b, from_z_a,
                  from_z_b, pieces,
                  staged, mixed, sent, landed, turned, column, summed_a, summed_b, final_a, final_b,
                  slab_sem, a2a_send, a2a_recv, gat_send, gat_recv, x_send, x_recv, z_send, z_recv, fin_send, fin_recv):
    ordered, from_x, from_z = (ordered_a, ordered_b), (from_x_a, from_x_b), (from_z_a, from_z_b)
    summed, final = (summed_a, summed_b), (final_a, final_b)
    p, v = lax.axis_index("pair"), lax.axis_index("virt")
    y, h, core = p // 4, (p // 2) % 2, p % 2
    z, xl = v // 2, v % 2

    def pair_of(dy, dh, dc):
        return (((y + dy) % 4) * 2 + (h + dh) % 2) * 2 + (core + dc) % 2

    up, down, across, sibling = pair_of(1, 0, 0), pair_of(3, 0, 0), pair_of(0, 1, 0), pair_of(0, 0, 1)

    def load(k):
        rows = pl.ds(pl.multiple_of(k * CHUNK * NB * SL, CHUNK * NB * SL), CHUNK * NB * SL)
        return pltpu.make_async_copy(integrals.at[rows], slab.at[rows], slab_sem.at[k])

    for k in range(RB // CHUNK):
        load(k).start()

    barrier = pltpu.get_barrier_semaphore()
    for q in (up, down, across, sibling):
        pl.semaphore_signal(barrier, inc=1, device_id=(q, v), device_id_type=MESH)
    for j in range(1, 16):
        pl.semaphore_signal(barrier, inc=1, device_id=(p, (v + j) % 16), device_id_type=MESH)

    @pl.when(p + v != 0)
    def _():
        pl.semaphore_signal(barrier, inc=1, device_id=(v, (p - v + 16) % 16), device_id_type=MESH)

    lane = lax.broadcasted_iota(jnp.int32, (1, BW), 1)

    def mate_size(block):
        mate, partner = pattern[block], 0
        for other in range(NB):
            partner = jnp.where(mate == other, sizes[other], partner)
        return partner

    mate_sizes = [mate_size(block) for block in range(NB)]

    def live(block, offset):
        return lane < jnp.where(v * SL + offset < sizes[block], mate_sizes[block], 0)

    def hop(f, slot, q, there, index):
        return pltpu.make_async_remote_copy(
            src_ref=gathered.at[f, core, slot], dst_ref=gathered.at[f, core, there],
            send_sem=gat_send.at[f, index], recv_sem=gat_recv.at[f, there], device_id=(q, v), device_id_type=MESH)

    def send_own(f):
        hop(f, 0, up, 1, 0).start()
        hop(f, 0, down, 2, 1).start()
        hop(f, 0, across, 3, 2).start()

    def arrived(f, slot):
        hop(f, slot, sibling, slot, 0).wait_recv()

    def share(f, far, from_core):
        slots = pl.ds(far * 4, 4)
        return pltpu.make_async_remote_copy(
            src_ref=gathered.at[f, from_core, slots], dst_ref=gathered.at[f, from_core, slots],
            send_sem=gat_send.at[f, 7 + far], recv_sem=gat_recv.at[f, 8 + far], device_id=(sibling, v),
            device_id_type=MESH)

    def near(f):
        arrived(f, 1)
        if f == 0:
            hop(f, 1, up, 6, 3).start()
        arrived(f, 2)
        if f == 1:
            hop(f, 2, down, 6, 3).start()
        arrived(f, 3)
        hop(f, 3, up, 4, 4).start()
        hop(f, 3, down, 5, 5).start()
        share(f, 0, core).start()

    def far(f):
        arrived(f, 6)
        hop(f, 6, across, 7, 6).start()
        arrived(f, 4)
        arrived(f, 5)
        arrived(f, 7)
        share(f, 1, core).start()

    def shared(f):
        for k in range(2):
            share(f, k, 1 - core).wait_recv()

    staged[...] = amp[...].astype(F32)

    shift = lax.broadcasted_iota(jnp.int32, (BW, WIN), 1) - lax.broadcasted_iota(jnp.int32, (BW, WIN), 0)
    depth = lax.broadcasted_iota(jnp.int32, (BW, WIN), 0)
    offset = 0
    for block in range(NB):
        inside = depth < mate_sizes[block]
        for odd in range(2):
            chosen = jnp.logical_and(inside, shift == offset + odd * (KP // 2 - (KP - WIN)))
            select[odd, pl.ds(block * BW, BW), :] = jnp.where(chosen, 1.0, 0.0).astype(BF)
        offset = offset + mate_sizes[block]

    def pack(source_ref, rows, put):
        def window(odd, part):
            first, last = REACH[odd][part]
            lanes = pl.ds(first * BW, (last - first) * BW)
            left = source_ref[odd, :, :, lanes].reshape(4 * rows, (last - first) * BW)
            right = select[odd, lanes, pl.ds(part * 256, 256)]
            return lax.dot_general(left, right, (((1,), (0,)), ((), ())), preferred_element_type=F32)

        def save(lane, value):
            value = value.astype(BF)
            for k in range(4):
                put(k, pl.ds(lane, value.shape[1]), value[k * rows:(k + 1) * rows])

        save(0, window(0, 0))
        save(256, window(0, 1))
        low = window(0, 2)
        save(512, low[:, :BW])
        high = window(1, 0)
        save(640, low[:, BW:] + high[:, :BW])
        save(768, high[:, BW:])
        save(896, window(1, 1))
        save(1152, window(1, 2))

    def pack_amplitudes(f):
        def put(k, lanes, value):
            gathered[f, core, 0, k, :, lanes] = value

        pack(few, QS, put)

    for c in range(SL):
        for block in range(NB):
            piece = staged[pl.ds(block * SL + c, QS, stride=NB * SL), :]
            piece = jnp.where(live(block, c), piece, 0.0).astype(BF)
            few[c % 2, c // 2, :, pl.ds(block * BW, BW)] = piece
    pack_amplitudes(0)

    group = lax.broadcasted_iota(jnp.int32, (SL, BW), 1) // SL

    def mix(block, carry):
        tiles = [staged[pl.ds(pl.multiple_of(q * NB * SL + block * SL, SL), SL), :] for q in range(QS)]
        for k in range(4):
            bit = 1 << k
            high = (group // bit) % 2 == 1
            new = list(tiles)
            for q in range(QS):
                if q & bit == 0:
                    new[q] = jnp.where(high, pltpu.roll(tiles[q | bit], SL * bit, 1), tiles[q])
                    new[q | bit] = jnp.where(high, tiles[q | bit], pltpu.roll(tiles[q], BW - SL * bit, 1))
            tiles = new
        for u in range(16):
            mixed[u, pl.ds(pl.multiple_of(block * SL, SL), SL), :] = tiles[u]
        return carry

    lax.fori_loop(0, NB, mix, 0)
    sent[...] = mixed[...].astype(BF)

    g = source[...]
    dy, dh = ((g >> 7) - y) & 3, ((g >> 6) - h) & 1
    slot = jnp.where(dy == 0, dh * 3, jnp.where(dy == 3, 1 + dh * 3, jnp.where(dy == 1, 2 + dh * 3, 6 + dh)))
    place = ((g & 1) * 256 + ((g >> 5) & 1) * 128 + slot * QS + ((g >> 1) & 15)).astype(F32)
    for k in range(4):
        column[pl.ds(k * BW, BW), :] = jnp.broadcast_to(place[k:k + 1, :], (BW, BW)).T.astype(jnp.int32)

    @pl.when(p + v != 0)
    def _():
        pl.semaphore_wait(barrier, 20)

    @pl.when(p + v == 0)
    def _():
        pl.semaphore_wait(barrier, 19)

    send_own(0)
    a2a = []
    for j in range(1, 16):
        u = (v + j) % 16
        copy = pltpu.make_async_remote_copy(
            src_ref=sent.at[u], dst_ref=landed.at[v], send_sem=a2a_send.at[j], recv_sem=a2a_recv.at[j],
            device_id=(p, u), device_id_type=MESH)
        copy.start()
        a2a.append(copy)
    landed[v] = sent[v]

    def relayout(k):
        rows = CHUNK * NB * SL
        w = slab[pl.ds(pl.multiple_of(k * rows, rows), rows), :].reshape(CHUNK, NB, SL, BW)
        for block in range(NB):
            t = jnp.swapaxes(w[:, block], 0, 1)
            for c in range(SL):
                narrow[c % 2, c // 2, :, pl.ds(block * BW, BW)] = t[c]

        def put(j, lanes, value):
            basis[j, pl.ds(pl.multiple_of(k * CHUNK, CHUNK), CHUNK), lanes] = value

        pack(narrow, CHUNK, put)

    def multiply(f):
        rows = pl.ds(f * 256, 256)

        def step(c, carry):
            left = gathered[f, :, :, c].reshape(256, KP)
            part = lax.dot_general(left, basis[c], (((1,), (1,)), ((), ())), preferred_element_type=F32)
            total[rows, :] = total[rows, :] + part
            return carry

        lax.fori_loop(0, 4, step, 0)

    def transposed():
        for copy in a2a:
            copy.wait()
        mixed[...] = landed[...].astype(F32)
        for block in range(NB):
            mate = pattern[block]
            tile = mixed[:, pl.ds(0, SL), :]
            for other in range(1, NB):
                tile = jnp.where(mate == other, mixed[:, pl.ds(other * SL, SL), :], tile)
            turned[...] = tile.reshape(BW, BW).T
            for c in range(SL):
                piece = turned[pl.ds(c, QS, stride=SL), :]
                piece = jnp.where(live(block, c), piece, 0.0).astype(BF)
                few[c % 2, c // 2, :, pl.ds(block * BW, BW)] = piece
        pack_amplitudes(1)
        send_own(1)

    def stage(k, carry):
        load(k).wait()
        relayout(k)

        @pl.when(k == 1)
        def _():
            near(0)

        @pl.when(k == 2)
        def _():
            transposed()

        @pl.when(k == 4)
        def _():
            far(0)

        return carry

    total[...] = jnp.zeros_like(total)
    lax.fori_loop(0, RB // CHUNK, stage, 0)
    shared(0)
    near(1)
    multiply(0)
    far(1)
    shared(1)
    multiply(1)

    for part in range(4):
        rows = pl.ds(part * 128, 128)
        whole = total[rows, :]
        high = whole.astype(BF)
        rest = whole - high.astype(F32)
        middle = rest.astype(BF)
        pieces[0, rows, :] = high
        pieces[1, rows, :] = middle
        pieces[2, rows, :] = (rest - middle.astype(F32)).astype(BF)

    order = [(z + dz) % 8 for dz in FAR + (0,)]

    def reorder(group, which, first, count):
        start, width = COLS[group]
        takes = []
        for u in order[first:first + count]:
            owner = u * 2 + (xl if which else 1 - xl)
            rows = pl.ds(pl.multiple_of((owner + p) % 16 * PD, PD), PD)
            takes.append(jnp.concatenate([jnp.where(column[rows, :] == lane + k * BW, 1.0, 0.0) for k in range(4)], axis=1))
        take = jnp.concatenate(takes, axis=0).astype(BF)
        lanes = pl.ds(start, width)
        rows = lax.dot_general(take, pieces[0, :, lanes], (((1,), (0,)), ((), ())), preferred_element_type=F32)
        for k in (1, 2):
            rows += lax.dot_general(take, pieces[k, :, lanes], (((1,), (0,)), ((), ())), preferred_element_type=F32)
        for j in range(count):
            ordered[group][which, first + j] = rows[j * PD:(j + 1) * PD]

    x_copies = [[], []]
    for group, count in ((0, 2), (1, 4)):
        for first in range(0, 8, 4):
            reorder(group, 0, first, 4)
            for j in range(first, first + 4, count):
                some = pl.ds(j, count)
                copy = pltpu.make_async_remote_copy(
                    src_ref=ordered[group].at[0, some], dst_ref=from_x[group].at[some], send_sem=x_send.at[group, j],
                    recv_sem=x_recv.at[group, j], device_id=(p, z * 2 + 1 - xl), device_id_type=MESH)
                copy.start()
                x_copies[group].append(copy)
    for group in range(2):
        for first in range(0, 8, 4):
            reorder(group, 1, first, 4)
    z_copies = [[], []]
    for group, count in ((0, 2), (1, 4)):
        for j, dz in enumerate(FAR + (0,)):
            if j % count == 0:
                x_copies[group][j // count].wait_recv()
            ordered[group][1, j] = ordered[group][1, j] + from_x[group][j]
            if dz:
                copy = pltpu.make_async_remote_copy(
                    src_ref=ordered[group].at[1, j], dst_ref=from_z[group].at[j], send_sem=z_send.at[group, j],
                    recv_sem=z_recv.at[group, j], device_id=(p, order[j] * 2 + xl), device_id_type=MESH)
                copy.start()
                z_copies[group].append(copy)

    def last(group):
        return pltpu.make_async_remote_copy(
            src_ref=summed[group], dst_ref=final[group], send_sem=fin_send.at[group], recv_sem=fin_recv.at[group],
            device_id=((p + v) % 16, p), device_id_type=MESH)

    for group in range(2):
        acc = ordered[group][1, 7]
        for j, copy in enumerate(z_copies[group]):
            copy.wait_recv()
            acc = acc + from_z[group][j]
        summed[group][...] = acc

        @pl.when(p + v != 0)
        def _():
            last(group).start()

        @pl.when(p + v == 0)
        def _():
            final[group][...] = summed[group][...]

    for group in range(2):
        @pl.when(p + v != 0)
        def _():
            last(group).wait()

        start, width = COLS[group]
        for i in range(start // BW, (start + width) // BW):
            row = v * RD + i
            live_width = 0
            for block in range(NB):
                here = jnp.where(row // NB < sizes[block], mate_sizes[block], 0)
                live_width = jnp.where(row % NB == block, here, live_width)
            piece = final[group][:, pl.ds(i * BW - start, BW)]
            out[:, pl.ds(i * BW, BW)] = jnp.where(lane < live_width, piece, 0.0)
    for copy in x_copies[0] + x_copies[1] + z_copies[0] + z_copies[1]:
        copy.wait_send()

    for f in range(2):
        for index in range(7):
            hop(f, 0, sibling, 0, index).wait_send()
        for k in range(2):
            share(f, k, core).wait_send()


def on_device(amplitudes, integrals, pattern, block_sizes, pair_source):
    vmem, smem = pl.BlockSpec(memory_space=pltpu.VMEM), pl.BlockSpec(memory_space=pltpu.SMEM)
    dma = pltpu.SemaphoreType.DMA
    result = pl.pallas_call(
        ladder_kernel,
        out_shape=jax.ShapeDtypeStruct((PD, RB), F32),
        in_specs=[vmem, pl.BlockSpec(memory_space=pl.ANY), smem, smem, vmem],
        out_specs=vmem,
        scratch_shapes=[
            pltpu.VMEM((RB * NB * SL, BW), BF),
            pltpu.VMEM((2, 4, CHUNK, LANES), BF),
            pltpu.VMEM((2, LANES, WIN), BF),
            pltpu.VMEM((2, 4, QS, LANES), BF),
            pltpu.VMEM((4, RB, KP), BF),
            pltpu.VMEM((2, 2, 8, 4, QS, KP), BF),
            pltpu.VMEM((512, RB), F32),
            *[pltpu.VMEM((2, 8, PD, width), F32) for _, width in COLS],
            *[pltpu.VMEM((8, PD, width), F32) for _, width in COLS],
            *[pltpu.VMEM((7, PD, width), F32) for _, width in COLS],
            pltpu.VMEM((3, 512, RB), BF),
            pltpu.VMEM((QS * NB * SL, BW), F32),
            pltpu.VMEM((16, NB * SL, BW), F32),
            pltpu.VMEM((16, NB * SL, BW), BF),
            pltpu.VMEM((16, NB * SL, BW), BF),
            pltpu.VMEM((BW, BW), F32),
            pltpu.VMEM((512, BW), jnp.int32),
            *[pltpu.VMEM((PD, width), F32) for _, width in COLS],
            *[pltpu.VMEM((PD, width), F32) for _, width in COLS],
            dma((RB // CHUNK,)),
            dma((16,)), dma((16,)),
            dma((2, 9)), dma((2, 10)),
            dma((2, 8)), dma((2, 8)), dma((2, 7)), dma((2, 7)),
            dma((2,)), dma((2,)),
        ],
        compiler_params=pltpu.CompilerParams(collective_id=0, has_side_effects=True, vmem_limit_bytes=60 * 2**20),
        cost_estimate=pl.CostEstimate(flops=2 * 512 * RB * 8192, bytes_accessed=14 * 2**20, transcendentals=0),
    )(amplitudes.reshape(QS * NB * SL, BW), integrals.reshape(RB * NB * SL, BW), pattern, block_sizes, pair_source.reshape(4, BW))
    return result.reshape(PD, RD, BW)


def solution(mesh):
    return jax.shard_map(
        on_device,
        mesh=mesh,
        in_specs=(P("pair", None, "virt", None), P("pair", None, None, "virt", None), P(), P(), P()),
        out_specs=P("pair", "virt", None),
        check_vma=False,
    )
```

```python
import functools

import jax
import jax.numpy as jnp
from jax import lax
from jax.experimental import pallas as pl
from jax.experimental.pallas import tpu as pltpu
from jax.sharding import PartitionSpec as P

MESH = pl.DeviceIdType.MESH
BF, F32 = jnp.bfloat16, jnp.float32
NB, SL, BW = 8, 8, 128
QS, PD, RD = 16, 32, 6
RB = RD * BW
CHUNK = 128
LANES = NB * BW
KP = 1408
WIN = 768
REACH = (((0, 6), (2, 8), (4, 8)), ((0, 6), (0, 8), (2, 8)))
FAR = (4, 3, 5, 2, 6, 1, 7)
COLS, BATCH = ((0, 512), (512, 256)), ((0, 2), (1, 4))


def ladder_kernel(amp, integrals, pattern, sizes, source, out, slab, narrow, select, few, basis, gathered, total, ordered_a, ordered_b, from_x_a, from_x_b, from_z_a,
                  from_z_b, pieces,
                  staged, mixed, sent, landed, turned, column, summed_a, summed_b, final_a, final_b,
                  slab_sem, a2a_send, a2a_recv, gat_send, gat_recv, x_send, x_recv, z_send, z_recv, fin_send, fin_recv):
    ordered, from_x, from_z = (ordered_a, ordered_b), (from_x_a, from_x_b), (from_z_a, from_z_b)
    summed, final = (summed_a, summed_b), (final_a, final_b)
    p, v = lax.axis_index("pair"), lax.axis_index("virt")
    y, h, core = p // 4, (p // 2) % 2, p % 2
    z, xl = v // 2, v % 2

    def pair_of(dy, dh, dc):
        return (((y + dy) % 4) * 2 + (h + dh) % 2) * 2 + (core + dc) % 2

    up, down, across, sibling = pair_of(1, 0, 0), pair_of(3, 0, 0), pair_of(0, 1, 0), pair_of(0, 0, 1)

    def load(k):
        rows = pl.ds(pl.multiple_of(k * CHUNK * NB * SL, CHUNK * NB * SL), CHUNK * NB * SL)
        return pltpu.make_async_copy(integrals.at[rows], slab.at[rows], slab_sem.at[k])

    for k in range(RB // CHUNK):
        load(k).start()

    barrier = pltpu.get_barrier_semaphore()
    for q in (up, down, across, sibling):
        pl.semaphore_signal(barrier, inc=1, device_id=(q, v), device_id_type=MESH)
    for j in range(1, 16):
        pl.semaphore_signal(barrier, inc=1, device_id=(p, (v + j) % 16), device_id_type=MESH)

    @pl.when(p + v != 0)
    def _():
        pl.semaphore_signal(barrier, inc=1, device_id=(v, (p - v + 16) % 16), device_id_type=MESH)

    lane = lax.broadcasted_iota(jnp.int32, (1, BW), 1)

    def mate_size(block):
        mate, partner = pattern[block], 0
        for other in range(NB):
            partner = jnp.where(mate == other, sizes[other], partner)
        return partner

    mate_sizes = [mate_size(block) for block in range(NB)]

    def live(block, offset):
        return lane < jnp.where(v * SL + offset < sizes[block], mate_sizes[block], 0)

    def hop(f, slot, q, there, index):
        return pltpu.make_async_remote_copy(
            src_ref=gathered.at[f, core, slot], dst_ref=gathered.at[f, core, there],
            send_sem=gat_send.at[f, index], recv_sem=gat_recv.at[f, there], device_id=(q, v), device_id_type=MESH)

    def send_own(f):
        hop(f, 0, up, 1, 0).start()
        hop(f, 0, down, 2, 1).start()
        hop(f, 0, across, 3, 2).start()

    def arrived(f, slot):
        hop(f, slot, sibling, slot, 0).wait_recv()

    def share(f, far, from_core):
        slots = pl.ds(far * 4, 4)
        return pltpu.make_async_remote_copy(
            src_ref=gathered.at[f, from_core, slots], dst_ref=gathered.at[f, from_core, slots],
            send_sem=gat_send.at[f, 7 + far], recv_sem=gat_recv.at[f, 8 + far], device_id=(sibling, v),
            device_id_type=MESH)

    def bend(f, half, slot, q):
        part = pl.ds(half * 2, 2)
        return pltpu.make_async_remote_copy(
            src_ref=gathered.at[f, core, slot, part], dst_ref=gathered.at[f, core, 6, part],
            send_sem=gat_send.at[f, 3 + half * 6], recv_sem=gat_recv.at[f, 6 - half * 6], device_id=(q, v),
            device_id_type=MESH)

    def near(f):
        arrived(f, 1)
        bend(f, 0, 1, up).start()
        arrived(f, 2)
        bend(f, 1, 2, down).start()
        arrived(f, 3)
        hop(f, 3, up, 4, 4).start()
        hop(f, 3, down, 5, 5).start()
        share(f, 0, core).start()

    def onward(f):
        for half in range(2):
            bend(f, half, 6, sibling).wait_recv()
        hop(f, 6, across, 7, 6).start()

    def far(f):
        arrived(f, 4)
        arrived(f, 5)
        arrived(f, 7)
        share(f, 1, core).start()

    def shared(f):
        for k in range(2):
            share(f, k, 1 - core).wait_recv()

    staged[...] = amp[...].astype(F32)

    shift = lax.broadcasted_iota(jnp.int32, (BW, WIN), 1) - lax.broadcasted_iota(jnp.int32, (BW, WIN), 0)
    depth = lax.broadcasted_iota(jnp.int32, (BW, WIN), 0)
    offset = 0
    for block in range(NB):
        inside = depth < mate_sizes[block]
        for odd in range(2):
            chosen = jnp.logical_and(inside, shift == offset + odd * (KP // 2 - (KP - WIN)))
            select[odd, pl.ds(block * BW, BW), :] = jnp.where(chosen, 1.0, 0.0).astype(BF)
        offset = offset + mate_sizes[block]

    def pack(source_ref, rows, put):
        def window(odd, part):
            first, last = REACH[odd][part]
            lanes = pl.ds(first * BW, (last - first) * BW)
            left = source_ref[odd, :, :, lanes].reshape(4 * rows, (last - first) * BW)
            right = select[odd, lanes, pl.ds(part * 256, 256)]
            return lax.dot_general(left, right, (((1,), (0,)), ((), ())), preferred_element_type=F32)

        def save(lane, value):
            value = value.astype(BF)
            for k in range(4):
                put(k, pl.ds(lane, value.shape[1]), value[k * rows:(k + 1) * rows])

        save(0, window(0, 0))
        save(256, window(0, 1))
        low = window(0, 2)
        save(512, low[:, :BW])
        high = window(1, 0)
        save(640, low[:, BW:] + high[:, :BW])
        save(768, high[:, BW:])
        save(896, window(1, 1))
        save(1152, window(1, 2))

    def pack_amplitudes(f):
        def put(k, lanes, value):
            gathered[f, core, 0, k, :, lanes] = value

        pack(few, QS, put)

    for c in range(SL):
        for block in range(NB):
            piece = staged[pl.ds(block * SL + c, QS, stride=NB * SL), :]
            piece = jnp.where(live(block, c), piece, 0.0).astype(BF)
            few[c % 2, c // 2, :, pl.ds(block * BW, BW)] = piece
    pack_amplitudes(0)

    group = lax.broadcasted_iota(jnp.int32, (SL, BW), 1) // SL

    def mix(block, carry):
        tiles = [staged[pl.ds(pl.multiple_of(q * NB * SL + block * SL, SL), SL), :] for q in range(QS)]
        for k in range(4):
            bit = 1 << k
            high = (group // bit) % 2 == 1
            new = list(tiles)
            for q in range(QS):
                if q & bit == 0:
                    new[q] = jnp.where(high, pltpu.roll(tiles[q | bit], SL * bit, 1), tiles[q])
                    new[q | bit] = jnp.where(high, tiles[q | bit], pltpu.roll(tiles[q], BW - SL * bit, 1))
            tiles = new
        for u in range(16):
            mixed[u, pl.ds(pl.multiple_of(block * SL, SL), SL), :] = tiles[u]
        return carry

    lax.fori_loop(0, NB, mix, 0)
    sent[...] = mixed[...].astype(BF)

    g = source[...]
    dy, dh = ((g >> 7) - y) & 3, ((g >> 6) - h) & 1
    slot = jnp.where(dy == 0, dh * 3, jnp.where(dy == 3, 1 + dh * 3, jnp.where(dy == 1, 2 + dh * 3, 6 + dh)))
    place = ((g & 1) * 256 + ((g >> 5) & 1) * 128 + slot * QS + ((g >> 1) & 15)).astype(F32)
    for k in range(4):
        column[pl.ds(k * BW, BW), :] = jnp.broadcast_to(place[k:k + 1, :], (BW, BW)).T.astype(jnp.int32)

    @pl.when(p + v != 0)
    def _():
        pl.semaphore_wait(barrier, 20)

    @pl.when(p + v == 0)
    def _():
        pl.semaphore_wait(barrier, 19)

    send_own(0)
    a2a = []
    for j in range(1, 16):
        u = (v + j) % 16
        copy = pltpu.make_async_remote_copy(
            src_ref=sent.at[u], dst_ref=landed.at[v], send_sem=a2a_send.at[j], recv_sem=a2a_recv.at[j],
            device_id=(p, u), device_id_type=MESH)
        copy.start()
        a2a.append(copy)
    landed[v] = sent[v]

    def relayout(k):
        rows = CHUNK * NB * SL
        w = slab[pl.ds(pl.multiple_of(k * rows, rows), rows), :].reshape(CHUNK, NB, SL, BW)
        for block in range(NB):
            t = jnp.swapaxes(w[:, block], 0, 1)
            for c in range(SL):
                narrow[c % 2, c // 2, :, pl.ds(block * BW, BW)] = t[c]

        def put(j, lanes, value):
            basis[j, pl.ds(pl.multiple_of(k * CHUNK, CHUNK), CHUNK), lanes] = value

        pack(narrow, CHUNK, put)

    def multiply(f, start, width):
        rows, lanes = pl.ds(f * 256, 256), pl.ds(start, width)

        def step(c, carry):
            left = gathered[f, :, :, c].reshape(256, KP)
            right = basis[c, lanes, :]
            part = lax.dot_general(left, right, (((1,), (1,)), ((), ())), preferred_element_type=F32)
            total[rows, lanes] = total[rows, lanes] + part
            return carry

        lax.fori_loop(0, 4, step, 0)

    def transposed():
        for copy in a2a:
            copy.wait()
        mixed[...] = landed[...].astype(F32)
        for block in range(NB):
            mate = pattern[block]
            tile = mixed[:, pl.ds(0, SL), :]
            for other in range(1, NB):
                tile = jnp.where(mate == other, mixed[:, pl.ds(other * SL, SL), :], tile)
            turned[...] = tile.reshape(BW, BW).T
            for c in range(SL):
                piece = turned[pl.ds(c, QS, stride=SL), :]
                piece = jnp.where(live(block, c), piece, 0.0).astype(BF)
                few[c % 2, c // 2, :, pl.ds(block * BW, BW)] = piece
        pack_amplitudes(1)
        send_own(1)

    def stage(k, carry):
        load(k).wait()
        relayout(k)

        @pl.when(k == 1)
        def _():
            near(0)

        @pl.when(k == 2)
        def _():
            transposed()

        @pl.when(k == 4)
        def _():
            onward(0)
            far(0)

        return carry

    total[...] = jnp.zeros_like(total)
    lax.fori_loop(0, RB // CHUNK, stage, 0)
    shared(0)
    near(1)
    multiply(0, 0, 512)
    onward(1)
    multiply(0, 512, 256)
    far(1)
    shared(1)

    def split(start, width):
        lanes = pl.ds(start, width)
        for part in range(4):
            rows = pl.ds(part * 128, 128)
            whole = total[rows, lanes]
            high = whole.astype(BF)
            rest = whole - high.astype(F32)
            middle = rest.astype(BF)
            pieces[0, rows, lanes] = high
            pieces[1, rows, lanes] = middle
            pieces[2, rows, lanes] = (rest - middle.astype(F32)).astype(BF)

    order = [(z + dz) % 8 for dz in FAR + (0,)]

    def reorder(group, which, first, count):
        start, width = COLS[group]
        takes = []
        for u in order[first:first + count]:
            owner = u * 2 + (xl if which else 1 - xl)
            rows = pl.ds(pl.multiple_of((owner + p) % 16 * PD, PD), PD)
            takes.append(jnp.concatenate([jnp.where(column[rows, :] == lane + k * BW, 1.0, 0.0) for k in range(4)], axis=1))
        take = jnp.concatenate(takes, axis=0).astype(BF)
        lanes = pl.ds(start, width)
        rows = lax.dot_general(take, pieces[0, :, lanes], (((1,), (0,)), ((), ())), preferred_element_type=F32)
        for k in (1, 2):
            rows += lax.dot_general(take, pieces[k, :, lanes], (((1,), (0,)), ((), ())), preferred_element_type=F32)
        for j in range(count):
            ordered[group][which, first + j] = rows[j * PD:(j + 1) * PD]

    x_copies = [[] for _ in COLS]
    for group, count in BATCH:
        multiply(1, *COLS[group])
        split(*COLS[group])
        for first in range(0, 8, 4):
            reorder(group, 0, first, 4)
            for j in range(first, first + 4, count):
                some = pl.ds(j, count)
                copy = pltpu.make_async_remote_copy(
                    src_ref=ordered[group].at[0, some], dst_ref=from_x[group].at[some], send_sem=x_send.at[group, j],
                    recv_sem=x_recv.at[group, j], device_id=(p, z * 2 + 1 - xl), device_id_type=MESH)
                copy.start()
                x_copies[group].append(copy)
    for group in range(len(COLS)):
        for first in range(0, 8, 4):
            reorder(group, 1, first, 4)
    z_copies = [[] for _ in COLS]
    for group, count in BATCH:
        for j, dz in enumerate(FAR + (0,)):
            if j % count == 0:
                x_copies[group][j // count].wait_recv()
            ordered[group][1, j] = ordered[group][1, j] + from_x[group][j]
            if dz:
                copy = pltpu.make_async_remote_copy(
                    src_ref=ordered[group].at[1, j], dst_ref=from_z[group].at[j], send_sem=z_send.at[group, j],
                    recv_sem=z_recv.at[group, j], device_id=(p, order[j] * 2 + xl), device_id_type=MESH)
                copy.start()
                z_copies[group].append(copy)

    def last(group):
        return pltpu.make_async_remote_copy(
            src_ref=summed[group], dst_ref=final[group], send_sem=fin_send.at[group], recv_sem=fin_recv.at[group],
            device_id=((p + v) % 16, p), device_id_type=MESH)

    for group in range(len(COLS)):
        acc = ordered[group][1, 7]
        for j, copy in enumerate(z_copies[group]):
            copy.wait_recv()
            acc = acc + from_z[group][j]
        summed[group][...] = acc

        @pl.when(p + v != 0)
        def _():
            last(group).start()

        @pl.when(p + v == 0)
        def _():
            final[group][...] = summed[group][...]

    for group in range(len(COLS)):
        @pl.when(p + v != 0)
        def _():
            last(group).wait()

        start, width = COLS[group]
        for i in range(start // BW, (start + width) // BW):
            row = v * RD + i
            live_width = 0
            for block in range(NB):
                here = jnp.where(row // NB < sizes[block], mate_sizes[block], 0)
                live_width = jnp.where(row % NB == block, here, live_width)
            piece = final[group][:, pl.ds(i * BW - start, BW)]
            out[:, pl.ds(i * BW, BW)] = jnp.where(lane < live_width, piece, 0.0)
    for copy in sum(x_copies + z_copies, []):
        copy.wait_send()

    for f in range(2):
        for index in (0, 1, 2, 4, 5, 6):
            hop(f, 0, sibling, 0, index).wait_send()
        for half in range(2):
            bend(f, half, 6, sibling).wait_send()
        for k in range(2):
            share(f, k, core).wait_send()


def on_device(amplitudes, integrals, pattern, block_sizes, pair_source):
    vmem, smem = pl.BlockSpec(memory_space=pltpu.VMEM), pl.BlockSpec(memory_space=pltpu.SMEM)
    dma = pltpu.SemaphoreType.DMA
    result = pl.pallas_call(
        ladder_kernel,
        out_shape=jax.ShapeDtypeStruct((PD, RB), F32),
        in_specs=[vmem, pl.BlockSpec(memory_space=pl.ANY), smem, smem, vmem],
        out_specs=vmem,
        scratch_shapes=[
            pltpu.VMEM((RB * NB * SL, BW), BF),
            pltpu.VMEM((2, 4, CHUNK, LANES), BF),
            pltpu.VMEM((2, LANES, WIN), BF),
            pltpu.VMEM((2, 4, QS, LANES), BF),
            pltpu.VMEM((4, RB, KP), BF),
            pltpu.VMEM((2, 2, 8, 4, QS, KP), BF),
            pltpu.VMEM((512, RB), F32),
            *[pltpu.VMEM((2, 8, PD, width), F32) for _, width in COLS],
            *[pltpu.VMEM((8, PD, width), F32) for _, width in COLS],
            *[pltpu.VMEM((7, PD, width), F32) for _, width in COLS],
            pltpu.VMEM((3, 512, RB), BF),
            pltpu.VMEM((QS * NB * SL, BW), F32),
            pltpu.VMEM((16, NB * SL, BW), F32),
            pltpu.VMEM((16, NB * SL, BW), BF),
            pltpu.VMEM((16, NB * SL, BW), BF),
            pltpu.VMEM((BW, BW), F32),
            pltpu.VMEM((512, BW), jnp.int32),
            *[pltpu.VMEM((PD, width), F32) for _, width in COLS],
            *[pltpu.VMEM((PD, width), F32) for _, width in COLS],
            dma((RB // CHUNK,)),
            dma((16,)), dma((16,)),
            dma((2, 10)), dma((2, 10)),
            dma((2, 8)), dma((2, 8)), dma((2, 7)), dma((2, 7)),
            dma((2,)), dma((2,)),
        ],
        compiler_params=pltpu.CompilerParams(collective_id=0, has_side_effects=True, vmem_limit_bytes=60 * 2**20),
        cost_estimate=pl.CostEstimate(flops=2 * 512 * RB * 8192, bytes_accessed=14 * 2**20, transcendentals=0),
    )(amplitudes.reshape(QS * NB * SL, BW), integrals.reshape(RB * NB * SL, BW), pattern, block_sizes, pair_source.reshape(4, BW))
    return result.reshape(PD, RD, BW)


def solution(mesh):
    return jax.shard_map(
        on_device,
        mesh=mesh,
        in_specs=(P("pair", None, "virt", None), P("pair", None, None, "virt", None), P(), P(), P()),
        out_specs=P("pair", "virt", None),
        check_vma=False,
    )
```

```python
import functools

import jax
import jax.numpy as jnp
from jax import lax
from jax.experimental import pallas as pl
from jax.experimental.pallas import tpu as pltpu
from jax.sharding import PartitionSpec as P

MESH = pl.DeviceIdType.MESH
BF, F32 = jnp.bfloat16, jnp.float32
NB, SL, BW = 8, 8, 128
QS, PD, RD = 16, 32, 6
RB = RD * BW
CHUNK = 128
LANES = NB * BW
KP = 1408
WIN = 768
REACH = (((0, 6), (2, 8), (4, 8)), ((0, 6), (0, 8), (2, 8)))
FAR = (4, 3, 5, 2, 6, 1, 7)
COLS, BATCH = ((0, 512), (512, 256)), ((0, 2), (1, 4))


def ladder_kernel(amp, integrals, pattern, sizes, source, out, slab, narrow, select, few, basis, gathered, total, ordered_a, ordered_b, from_x_a, from_x_b, from_z_a,
                  from_z_b, pieces,
                  staged, mixed, sent, landed, turned, column, summed_a, summed_b, final_a, final_b,
                  slab_sem, a2a_send, a2a_recv, gat_send, gat_recv, x_send, x_recv, z_send, z_recv, fin_send, fin_recv):
    ordered, from_x, from_z = (ordered_a, ordered_b), (from_x_a, from_x_b), (from_z_a, from_z_b)
    summed, final = (summed_a, summed_b), (final_a, final_b)
    p, v = lax.axis_index("pair"), lax.axis_index("virt")
    y, h, core = p // 4, (p // 2) % 2, p % 2
    z, xl = v // 2, v % 2

    def pair_of(dy, dh, dc):
        return (((y + dy) % 4) * 2 + (h + dh) % 2) * 2 + (core + dc) % 2

    up, down, across, sibling = pair_of(1, 0, 0), pair_of(3, 0, 0), pair_of(0, 1, 0), pair_of(0, 0, 1)

    def load(k):
        rows = pl.ds(pl.multiple_of(k * CHUNK * NB * SL, CHUNK * NB * SL), CHUNK * NB * SL)
        return pltpu.make_async_copy(integrals.at[rows], slab.at[rows], slab_sem.at[k])

    for k in range(RB // CHUNK):
        load(k).start()

    barrier = pltpu.get_barrier_semaphore()
    for q in (up, down, across, sibling):
        pl.semaphore_signal(barrier, inc=1, device_id=(q, v), device_id_type=MESH)
    for j in range(1, 16):
        pl.semaphore_signal(barrier, inc=1, device_id=(p, (v + j) % 16), device_id_type=MESH)

    @pl.when(p + v != 0)
    def _():
        pl.semaphore_signal(barrier, inc=1, device_id=(v, (p - v + 16) % 16), device_id_type=MESH)

    lane = lax.broadcasted_iota(jnp.int32, (1, BW), 1)

    def mate_size(block):
        mate, partner = pattern[block], 0
        for other in range(NB):
            partner = jnp.where(mate == other, sizes[other], partner)
        return partner

    mate_sizes = [mate_size(block) for block in range(NB)]

    def live(block, offset):
        return lane < jnp.where(v * SL + offset < sizes[block], mate_sizes[block], 0)

    def hop(f, slot, q, there, index):
        return pltpu.make_async_remote_copy(
            src_ref=gathered.at[f, core, slot], dst_ref=gathered.at[f, core, there],
            send_sem=gat_send.at[f, index], recv_sem=gat_recv.at[f, there], device_id=(q, v), device_id_type=MESH)

    def send_own(f):
        hop(f, 0, up, 1, 0).start()
        hop(f, 0, down, 2, 1).start()
        hop(f, 0, across, 3, 2).start()

    def arrived(f, slot):
        hop(f, slot, sibling, slot, 0).wait_recv()

    def share(f, far, from_core):
        slots = pl.ds(far * 4, 4)
        return pltpu.make_async_remote_copy(
            src_ref=gathered.at[f, from_core, slots], dst_ref=gathered.at[f, from_core, slots],
            send_sem=gat_send.at[f, 7 + far], recv_sem=gat_recv.at[f, 8 + far], device_id=(sibling, v),
            device_id_type=MESH)

    def bend(f, half, slot, q):
        part = pl.ds(half * 2, 2)
        return pltpu.make_async_remote_copy(
            src_ref=gathered.at[f, core, slot, part], dst_ref=gathered.at[f, core, 6, part],
            send_sem=gat_send.at[f, 3 + half * 6], recv_sem=gat_recv.at[f, 6 - half * 6], device_id=(q, v),
            device_id_type=MESH)

    def near(f):
        arrived(f, 1)
        bend(f, 0, 1, up).start()
        arrived(f, 2)
        bend(f, 1, 2, down).start()
        arrived(f, 3)
        hop(f, 3, up, 4, 4).start()
        hop(f, 3, down, 5, 5).start()
        share(f, 0, core).start()

    def onward(f):
        for half in range(2):
            bend(f, half, 6, sibling).wait_recv()
        hop(f, 6, across, 7, 6).start()

    def far(f):
        arrived(f, 4)
        arrived(f, 5)
        arrived(f, 7)
        share(f, 1, core).start()

    def shared(f):
        for k in range(2):
            share(f, k, 1 - core).wait_recv()

    staged[...] = amp[...].astype(F32)

    shift = lax.broadcasted_iota(jnp.int32, (BW, WIN), 1) - lax.broadcasted_iota(jnp.int32, (BW, WIN), 0)
    depth = lax.broadcasted_iota(jnp.int32, (BW, WIN), 0)
    offset = 0
    for block in range(NB):
        inside = depth < mate_sizes[block]
        for odd in range(2):
            chosen = jnp.logical_and(inside, shift == offset + odd * (KP // 2 - (KP - WIN)))
            select[odd, pl.ds(block * BW, BW), :] = jnp.where(chosen, 1.0, 0.0).astype(BF)
        offset = offset + mate_sizes[block]

    def pack(source_ref, rows, put):
        def window(odd, part):
            first, last = REACH[odd][part]
            lanes = pl.ds(first * BW, (last - first) * BW)
            left = source_ref[odd, :, :, lanes].reshape(4 * rows, (last - first) * BW)
            right = select[odd, lanes, pl.ds(part * 256, 256)]
            return lax.dot_general(left, right, (((1,), (0,)), ((), ())), preferred_element_type=F32)

        def save(lane, value):
            value = value.astype(BF)
            for k in range(4):
                put(k, pl.ds(lane, value.shape[1]), value[k * rows:(k + 1) * rows])

        save(0, window(0, 0))
        save(256, window(0, 1))
        low = window(0, 2)
        save(512, low[:, :BW])
        high = window(1, 0)
        save(640, low[:, BW:] + high[:, :BW])
        save(768, high[:, BW:])
        save(896, window(1, 1))
        save(1152, window(1, 2))

    def pack_amplitudes(f):
        def put(k, lanes, value):
            gathered[f, core, 0, k, :, lanes] = value

        pack(few, QS, put)

    for c in range(SL):
        for block in range(NB):
            piece = staged[pl.ds(block * SL + c, QS, stride=NB * SL), :]
            piece = jnp.where(live(block, c), piece, 0.0).astype(BF)
            few[c % 2, c // 2, :, pl.ds(block * BW, BW)] = piece
    pack_amplitudes(0)

    group = lax.broadcasted_iota(jnp.int32, (SL, BW), 1) // SL

    def mix(block, carry):
        tiles = [staged[pl.ds(pl.multiple_of(q * NB * SL + block * SL, SL), SL), :] for q in range(QS)]
        for k in range(4):
            bit = 1 << k
            high = (group // bit) % 2 == 1
            new = list(tiles)
            for q in range(QS):
                if q & bit == 0:
                    new[q] = jnp.where(high, pltpu.roll(tiles[q | bit], SL * bit, 1), tiles[q])
                    new[q | bit] = jnp.where(high, tiles[q | bit], pltpu.roll(tiles[q], BW - SL * bit, 1))
            tiles = new
        for u in range(16):
            mixed[u, pl.ds(pl.multiple_of(block * SL, SL), SL), :] = tiles[u]
        return carry

    lax.fori_loop(0, NB, mix, 0)
    sent[...] = mixed[...].astype(BF)

    g = source[...]
    dy, dh = ((g >> 7) - y) & 3, ((g >> 6) - h) & 1
    slot = jnp.where(dy == 0, dh * 3, jnp.where(dy == 3, 1 + dh * 3, jnp.where(dy == 1, 2 + dh * 3, 6 + dh)))
    place = ((g & 1) * 256 + ((g >> 5) & 1) * 128 + slot * QS + ((g >> 1) & 15)).astype(F32)
    for k in range(4):
        column[pl.ds(k * BW, BW), :] = jnp.broadcast_to(place[k:k + 1, :], (BW, BW)).T.astype(jnp.int32)

    @pl.when(p + v != 0)
    def _():
        pl.semaphore_wait(barrier, 20)

    @pl.when(p + v == 0)
    def _():
        pl.semaphore_wait(barrier, 19)

    send_own(0)
    a2a = []
    for j in range(1, 16):
        u = (v + j) % 16
        copy = pltpu.make_async_remote_copy(
            src_ref=sent.at[u], dst_ref=landed.at[v], send_sem=a2a_send.at[j], recv_sem=a2a_recv.at[j],
            device_id=(p, u), device_id_type=MESH)
        copy.start()
        a2a.append(copy)
    landed[v] = sent[v]

    def relayout(k):
        rows = CHUNK * NB * SL
        w = slab[pl.ds(pl.multiple_of(k * rows, rows), rows), :].reshape(CHUNK, NB, SL, BW)
        for block in range(NB):
            t = jnp.swapaxes(w[:, block], 0, 1)
            for c in range(SL):
                narrow[c % 2, c // 2, :, pl.ds(block * BW, BW)] = t[c]

        def put(j, lanes, value):
            basis[j, pl.ds(pl.multiple_of(k * CHUNK, CHUNK), CHUNK), lanes] = value

        pack(narrow, CHUNK, put)

    def multiply(f, start, width):
        rows, lanes = pl.ds(f * 256, 256), pl.ds(start, width)

        def step(c, carry):
            left = gathered[f, :, :, c].reshape(256, KP)
            right = basis[c, lanes, :]
            part = lax.dot_general(left, right, (((1,), (1,)), ((), ())), preferred_element_type=F32)
            total[rows, lanes] = total[rows, lanes] + part
            return carry

        lax.fori_loop(0, 4, step, 0)

    def transposed():
        for copy in a2a:
            copy.wait()
        mixed[...] = landed[...].astype(F32)
        for block in range(NB):
            mate = pattern[block]
            tile = mixed[:, pl.ds(0, SL), :]
            for other in range(1, NB):
                tile = jnp.where(mate == other, mixed[:, pl.ds(other * SL, SL), :], tile)
            turned[...] = tile.reshape(BW, BW).T
            for c in range(SL):
                piece = turned[pl.ds(c, QS, stride=SL), :]
                piece = jnp.where(live(block, c), piece, 0.0).astype(BF)
                few[c % 2, c // 2, :, pl.ds(block * BW, BW)] = piece
        pack_amplitudes(1)
        send_own(1)

    def stage(k, carry):
        load(k).wait()
        relayout(k)

        @pl.when(k == 1)
        def _():
            near(0)

        @pl.when(k == 2)
        def _():
            transposed()

        @pl.when(k == 4)
        def _():
            onward(0)
            far(0)

        return carry

    total[...] = jnp.zeros_like(total)
    lax.fori_loop(0, RB // CHUNK, stage, 0)
    shared(0)
    near(1)
    multiply(0, 0, 512)
    onward(1)
    multiply(0, 512, 256)
    far(1)
    shared(1)

    def split(start, width):
        lanes = pl.ds(start, width)
        for part in range(4):
            rows = pl.ds(part * 128, 128)
            whole = total[rows, lanes]
            high = whole.astype(BF)
            rest = whole - high.astype(F32)
            middle = rest.astype(BF)
            pieces[0, rows, lanes] = high
            pieces[1, rows, lanes] = middle
            pieces[2, rows, lanes] = (rest - middle.astype(F32)).astype(BF)

    order = [(z + dz) % 8 for dz in FAR + (0,)]

    def reorder(group, which, first, count):
        start, width = COLS[group]
        takes = []
        for u in order[first:first + count]:
            owner = u * 2 + (xl if which else 1 - xl)
            rows = pl.ds(pl.multiple_of((owner + p) % 16 * PD, PD), PD)
            takes.append(jnp.concatenate([jnp.where(column[rows, :] == lane + k * BW, 1.0, 0.0) for k in range(4)], axis=1))
        take = jnp.concatenate(takes, axis=0).astype(BF)
        lanes = pl.ds(start, width)
        rows = lax.dot_general(take, pieces[0, :, lanes], (((1,), (0,)), ((), ())), preferred_element_type=F32)
        for k in (1, 2):
            rows += lax.dot_general(take, pieces[k, :, lanes], (((1,), (0,)), ((), ())), preferred_element_type=F32)
        for j in range(count):
            ordered[group][which, first + j] = rows[j * PD:(j + 1) * PD]

    x_copies = [[] for _ in COLS]
    for group, count in BATCH:
        multiply(1, *COLS[group])
        split(*COLS[group])
        for first in range(0, 8, 4):
            reorder(group, 0, first, 4)
            for j in range(first, first + 4, count):
                some = pl.ds(j, count)
                copy = pltpu.make_async_remote_copy(
                    src_ref=ordered[group].at[0, some], dst_ref=from_x[group].at[some], send_sem=x_send.at[group, j],
                    recv_sem=x_recv.at[group, j], device_id=(p, z * 2 + 1 - xl), device_id_type=MESH)
                copy.start()
                x_copies[group].append(copy)
    for group in range(len(COLS)):
        for first in range(0, 8, 4):
            reorder(group, 1, first, 4)
    z_copies = [[] for _ in COLS]
    for group, count in BATCH:
        for j, dz in enumerate(FAR + (0,)):
            if j % count == 0:
                x_copies[group][j // count].wait_recv()
            ordered[group][1, j] = ordered[group][1, j] + from_x[group][j]
            if dz:
                copy = pltpu.make_async_remote_copy(
                    src_ref=ordered[group].at[1, j], dst_ref=from_z[group].at[j], send_sem=z_send.at[group, j],
                    recv_sem=z_recv.at[group, j], device_id=(p, order[j] * 2 + xl), device_id_type=MESH)
                copy.start()
                z_copies[group].append(copy)

    def last(group):
        return pltpu.make_async_remote_copy(
            src_ref=summed[group], dst_ref=final[group], send_sem=fin_send.at[group], recv_sem=fin_recv.at[group],
            device_id=((p + v) % 16, p), device_id_type=MESH)

    for group in range(len(COLS)):
        acc = ordered[group][1, 7]
        for j, copy in enumerate(z_copies[group]):
            copy.wait_recv()
            acc = acc + from_z[group][j]
        summed[group][...] = acc

        @pl.when(p + v != 0)
        def _():
            last(group).start()

        @pl.when(p + v == 0)
        def _():
            final[group][...] = summed[group][...]

    for group in range(len(COLS)):
        @pl.when(p + v != 0)
        def _():
            last(group).wait()

        start, width = COLS[group]
        for i in range(start // BW, (start + width) // BW):
            row = v * RD + i
            live_width = 0
            for block in range(NB):
                here = jnp.where(row // NB < sizes[block], mate_sizes[block], 0)
                live_width = jnp.where(row % NB == block, here, live_width)
            piece = final[group][:, pl.ds(i * BW - start, BW)]
            out[i] = jnp.where(lane < live_width, piece, 0.0)
    for copy in sum(x_copies + z_copies, []):
        copy.wait_send()

    for f in range(2):
        for index in (0, 1, 2, 4, 5, 6):
            hop(f, 0, sibling, 0, index).wait_send()
        for half in range(2):
            bend(f, half, 6, sibling).wait_send()
        for k in range(2):
            share(f, k, core).wait_send()


def on_device(amplitudes, integrals, pattern, block_sizes, pair_source):
    vmem, smem = pl.BlockSpec(memory_space=pltpu.VMEM), pl.BlockSpec(memory_space=pltpu.SMEM)
    dma = pltpu.SemaphoreType.DMA
    result = pl.pallas_call(
        ladder_kernel,
        out_shape=jax.ShapeDtypeStruct((RD, PD, BW), F32),
        in_specs=[vmem, pl.BlockSpec(memory_space=pl.ANY), smem, smem, vmem],
        out_specs=vmem,
        scratch_shapes=[
            pltpu.VMEM((RB * NB * SL, BW), BF),
            pltpu.VMEM((2, 4, CHUNK, LANES), BF),
            pltpu.VMEM((2, LANES, WIN), BF),
            pltpu.VMEM((2, 4, QS, LANES), BF),
            pltpu.VMEM((4, RB, KP), BF),
            pltpu.VMEM((2, 2, 8, 4, QS, KP), BF),
            pltpu.VMEM((512, RB), F32),
            *[pltpu.VMEM((2, 8, PD, width), F32) for _, width in COLS],
            *[pltpu.VMEM((8, PD, width), F32) for _, width in COLS],
            *[pltpu.VMEM((7, PD, width), F32) for _, width in COLS],
            pltpu.VMEM((3, 512, RB), BF),
            pltpu.VMEM((QS * NB * SL, BW), F32),
            pltpu.VMEM((16, NB * SL, BW), F32),
            pltpu.VMEM((16, NB * SL, BW), BF),
            pltpu.VMEM((16, NB * SL, BW), BF),
            pltpu.VMEM((BW, BW), F32),
            pltpu.VMEM((512, BW), jnp.int32),
            *[pltpu.VMEM((PD, width), F32) for _, width in COLS],
            *[pltpu.VMEM((PD, width), F32) for _, width in COLS],
            dma((RB // CHUNK,)),
            dma((16,)), dma((16,)),
            dma((2, 10)), dma((2, 10)),
            dma((2, 8)), dma((2, 8)), dma((2, 7)), dma((2, 7)),
            dma((2,)), dma((2,)),
        ],
        compiler_params=pltpu.CompilerParams(collective_id=0, has_side_effects=True, vmem_limit_bytes=60 * 2**20),
        cost_estimate=pl.CostEstimate(flops=2 * 512 * RB * 8192, bytes_accessed=14 * 2**20, transcendentals=0),
    )(amplitudes.reshape(QS * NB * SL, BW), integrals.reshape(RB * NB * SL, BW), pattern, block_sizes, pair_source.reshape(4, BW))
    return result.transpose(1, 0, 2)


def solution(mesh):
    return jax.shard_map(
        on_device,
        mesh=mesh,
        in_specs=(P("pair", None, "virt", None), P("pair", None, None, "virt", None), P(), P(), P()),
        out_specs=P("pair", "virt", None),
        check_vma=False,
    )
```
